256 devices in a mesh: cfg: 2 (over core), pipe: 8 (over z), sp: 16 (over x, y).
Axes of the slice: x: 4, y: 4, z: 8, core: 2. Of those that a mesh axis runs over, the one named last changes fastest.
Arguments:
- hidden: bfloat16 [2, 8, 1024, 5120], P('cfg', 'pipe', 'sp'), may hold values from -1.5 to 1.5
- query: bfloat16 [2, 8, 1024, 4096], P('cfg', 'pipe', 'sp'), may hold values from -16 to 16
- key_new: bfloat16 [2, 8, 1024, 4096], P('cfg', 'pipe', 'sp'), may hold values from -9.6 to 9.6
- value_new: bfloat16 [2, 8, 1024, 4096], P('cfg', 'pipe', 'sp'), may hold values from -6 to 6
- stale_key: bfloat16 [2, 8, 7168, 4096], P('cfg', 'pipe', None, 'sp'), may hold values from -9.5625 to 9.5625
- stale_value: bfloat16 [2, 8, 7168, 4096], P('cfg', 'pipe', None, 'sp'), may hold values from -6 to 6
- out_weight: bfloat16 [8, 4096, 5120], P('pipe', None, 'sp'), may hold values from -0.09375 to 0.09375
Outputs:
- next_input: bfloat16 [2, 8, 1024, 5120], P('cfg', 'pipe', 'sp')
- guided: bfloat16 [8, 1024, 5120], P('pipe', 'sp', 'cfg')
The draws below stay inside these ranges and needn't reach their ends.
All inputs are finite; a program needn't handle non-finite values.
Results may differ from the reference program's by a relative error of at most 0.014.
Values may be sent and summed in bfloat16 or wider, within the bound.
A program may use at most 128 MiB of HBM per device.

```python
import jax
import jax.numpy as jnp
from jax import lax

D = 5120
HEAD_DIM = 128
SECTIONS = 8
PATCH = 1024
OTHERS = 7168
HD = 4096


def drawn_rows(key):
    return jnp.clip(jax.random.normal(key, (2, SECTIONS, PATCH, HD), jnp.float32), -6.0, 6.0) * 1.6


def draw_query(key, part):
    key = jax.random.fold_in(key, 11)
    values = drawn_rows(key)
    return values.astype(jnp.bfloat16)


def draw_key_new(key, part):
    key = jax.random.fold_in(key, 12)
    values = drawn_rows(key)
    return values.astype(jnp.bfloat16)


def block_scale(rng, shape, shards, smallest, largest):
    level = 1.0
    for position, parts in shards:
        draws = jax.random.uniform(jax.random.fold_in(jax.random.fold_in(rng, 6), position), (parts,), jnp.float32, smallest / len(shards), largest / len(shards))
        level = level * jnp.repeat(jnp.exp(draws), shape[position] // parts).reshape((-1,) + (1,) * (len(shape) - 1 - position))
    return level


def noise(own_key, shape, deviation, reach, cuts=(), kind=jnp.bfloat16):
    factor_of = block_scale(own_key, shape, cuts, -0.22, 0.18) if cuts else 1.0
    entries = jax.random.normal(own_key, shape, jnp.float32) * deviation * factor_of
    return jnp.minimum(jnp.maximum(entries, -reach), reach).astype(kind)


def setup_inputs(seed: int = 0) -> dict:
    key_of = jax.random.split(jax.random.key(seed), 8)
    return {
        "hidden": noise(key_of[0], (2, SECTIONS, PATCH, D), 0.25, 1.5, ((0, 2), (1, 8), (2, 16))),
        "query": draw_query(jax.random.fold_in(key_of[7], 71), 0),
        "key_new": draw_key_new(jax.random.fold_in(key_of[7], 71), 0),
        "value_new": noise(key_of[3], (2, SECTIONS, PATCH, HD), 1.0, 6.0, ((0, 2), (1, 8), (2, 16))),
        "stale_key": noise(key_of[4], (2, SECTIONS, OTHERS, HD), 1.6, 9.5625, ((0, 2), (1, 8), (3, 16))),
        "stale_value": noise(key_of[5], (2, SECTIONS, OTHERS, HD), 1.0, 6.0, ((0, 2), (1, 8), (3, 16))),
        "out_weight": noise(key_of[6], (SECTIONS, HD, D), HD ** -0.5, 0.09375, ((0, 8), (2, 16))),
    }


guidance_scale = 5.0


def attention(query_rows, key_rows, value_rows):
    count = query_rows.shape[0]
    heads = query_rows.shape[1] // HEAD_DIM
    scale = 1.0 / (HEAD_DIM ** 0.5)
    q_heads = query_rows.reshape(count, heads, HEAD_DIM).transpose(1, 0, 2)
    k_heads = key_rows.reshape(-1, heads, HEAD_DIM).transpose(1, 0, 2)
    v_heads = value_rows.reshape(-1, heads, HEAD_DIM).transpose(1, 0, 2)

    def one_head(operands):
        q_one, k_one, v_one = operands
        scores = jnp.dot(q_one, k_one.T, preferred_element_type=jnp.float32) * scale
        weights = jnp.exp(scores - jnp.max(scores, axis=-1, keepdims=True))
        total = jnp.sum(weights, axis=-1, keepdims=True)
        mixed = jnp.dot(weights.astype(jnp.bfloat16), v_one, preferred_element_type=jnp.float32) / total
        return mixed.astype(jnp.bfloat16)

    attended = lax.map(one_head, (q_heads, k_heads, v_heads))
    return attended.transpose(1, 0, 2).reshape(count, heads * HEAD_DIM)


def reference(hidden, query, key_new, value_new, stale_key, stale_value, out_weight):
    halves = []
    for half in range(2):
        sections = []
        for section in range(SECTIONS):
            keys = jnp.concatenate([key_new[half, section], stale_key[half, section]], axis=0)
            values = jnp.concatenate([value_new[half, section], stale_value[half, section]], axis=0)
            attended = attention(query[half, section], keys, values)
            projected = jnp.dot(attended, out_weight[section], preferred_element_type=jnp.float32)
            sections.append((hidden[half, section].astype(jnp.float32) + projected).astype(jnp.bfloat16))
        halves.append(jnp.stack(sections))
    block_out = jnp.stack(halves)
    next_input = jnp.roll(block_out, 1, axis=1)
    cond = block_out[0].astype(jnp.float32)
    uncond = block_out[1].astype(jnp.float32)
    guided = (uncond + guidance_scale * (cond - uncond)).astype(jnp.bfloat16)
    return next_input, guided
```

```python
import jax
import jax.numpy as jnp
from jax import lax
from jax.experimental import pallas as pl
from jax.experimental.pallas import tpu as pltpu
from jax.sharding import PartitionSpec as P

HEAD_DIM = 128


guidance_scale = 5.0


def from_behind(array, axis, by):
    devices = lax.axis_size(axis)
    return lax.ppermute(array, axis, [(i, (i + by) % devices) for i in range(devices)])


def from_partner(array, axis, bit):
    return lax.ppermute(array, axis, [(i, i ^ 1 << bit) for i in range(lax.axis_size(axis))])


SCALE = 1.4426950408889634 / HEAD_DIM**0.5
Q_BLOCK = 256
K_BLOCK = 1024


def attend_kernel(q_ref, k_new, v_new, k_old, v_old, o_ref):
    blocks = 1 + k_old.shape[0] // K_BLOCK

    def one_block(i, carry):
        rows = pl.ds(pl.multiple_of(i * Q_BLOCK, Q_BLOCK), Q_BLOCK)
        for h in range(q_ref.shape[1] // HEAD_DIM):
            cols = slice(h * HEAD_DIM, (h + 1) * HEAD_DIM)
            scaled = q_ref[rows, cols].astype(jnp.float32) * SCALE
            high = scaled.astype(jnp.bfloat16)
            low = (scaled - high.astype(jnp.float32)).astype(jnp.bfloat16)
            q = jnp.concatenate([high, low], axis=1)
            top = acc = None
            for j in range(blocks):
                if j == 0:
                    k, v = k_new[:, cols], v_new[:, cols]
                else:
                    part = slice((j - 1) * K_BLOCK, j * K_BLOCK)
                    k, v = k_old[part, cols], v_old[part, cols]
                s = lax.dot_general(
                    q,
                    jnp.concatenate([k, k], axis=1),
                    (((1,), (1,)), ((), ())),
                    preferred_element_type=jnp.float32,
                )
                here = jnp.max(s, axis=1, keepdims=True)
                peak = here if top is None else jnp.maximum(top, here)
                w = jnp.exp2(s - peak).astype(jnp.bfloat16)
                both = jnp.concatenate([v, jnp.ones_like(v)], axis=1)
                r = jnp.dot(w, both, preferred_element_type=jnp.float32)
                acc = r if top is None else acc * jnp.exp2(top - peak) + r
                top = peak
            out = acc[:, :HEAD_DIM] / acc[:, HEAD_DIM:]
            o_ref[rows, cols] = out.astype(jnp.bfloat16)
        return carry

    lax.fori_loop(0, q_ref.shape[0] // Q_BLOCK, one_block, 0)


def attend(q, k_new, v_new, k_old, v_old):
    return pl.pallas_call(
        attend_kernel,
        out_shape=jax.ShapeDtypeStruct(q.shape, jnp.bfloat16),
        in_specs=[pl.BlockSpec(memory_space=pltpu.VMEM)] * 5,
        out_specs=pl.BlockSpec(memory_space=pltpu.VMEM),
        compiler_params=pltpu.CompilerParams(vmem_limit_bytes=48 * 2**20),
    )(q, k_new, v_new, k_old, v_old)


def on_device(hidden, query, key_new, value_new, stale_key, stale_value, out_weight):
    q_tokens = query[0, 0]
    k_tokens = key_new[0, 0]
    v_tokens = value_new[0, 0]
    q_all = lax.all_to_all(q_tokens, "sp", split_axis=1, concat_axis=0, tiled=True)
    k_all, v_all = (
        lax.all_to_all(k_tokens, "sp", split_axis=1, concat_axis=0, tiled=True),
        lax.all_to_all(v_tokens, "sp", split_axis=1, concat_axis=0, tiled=True),
    )
    attended = attend(q_all, k_all, v_all, stale_key[0, 0], stale_value[0, 0])
    weight = out_weight[0]
    features = lax.all_gather(attended, "sp", axis=1, tiled=True)
    columns = jnp.dot(features, weight, preferred_element_type=jnp.float32)
    projected = lax.all_to_all(
        columns.astype(jnp.bfloat16), "sp", split_axis=0, concat_axis=1, tiled=True
    ).astype(columns.dtype)
    block_out = (hidden[0, 0].astype(jnp.float32) + projected).astype(jnp.bfloat16)
    handed = from_behind(block_out, "pipe", 1)
    half_width = block_out.shape[1] // 2
    mine = lax.axis_index("cfg")
    outgoing = lax.dynamic_slice_in_dim(block_out, (1 - mine) * half_width, half_width, 1)
    own_part = lax.dynamic_slice_in_dim(block_out, mine * half_width, half_width, 1)
    partner = from_partner(outgoing, "cfg", 0)
    is_first = mine == 0
    cond = jnp.where(is_first, own_part, partner).astype(jnp.float32)
    uncond = jnp.where(is_first, partner, own_part).astype(jnp.float32)
    guided = (uncond + guidance_scale * (cond - uncond)).astype(jnp.bfloat16)
    return (handed[None, None], guided[None])


def solution(mesh):
    return jax.shard_map(
        on_device,
        mesh=mesh,
        in_specs=(
            P("cfg", "pipe", "sp", None),
            P("cfg", "pipe", "sp", None),
            P("cfg", "pipe", "sp", None),
            P("cfg", "pipe", "sp", None),
            P("cfg", "pipe", None, "sp"),
            P("cfg", "pipe", None, "sp"),
            P("pipe", None, "sp"),
        ),
        out_specs=(P("cfg", "pipe", "sp", None), P("pipe", "sp", "cfg")),
        check_vma=False,
    )
```

```python
import functools

import jax
import jax.numpy as jnp
from jax import lax
from jax.experimental import pallas as pl
from jax.experimental.pallas import tpu as pltpu
from jax.sharding import PartitionSpec as P

HEAD_DIM = 128
SCALE = 1.4426950408889634 / HEAD_DIM**0.5
GUIDANCE = 5.0
MESH = pl.DeviceIdType.MESH
SIDE = 4
PEERS = SIDE * SIDE
BLOCKS = 4
OWN = 16
ROWS = PEERS * OWN
FEAT = 256
WIDE = SIDE * FEAT
SLICE = 320
COLS = SIDE * SLICE
MODEL = PEERS * SLICE
HALF = MODEL // 2
FRESH = 1024
STALE = 7168
K_BLOCK = 1024


def remote(src, dst, send, recv, **to):
    return pltpu.make_async_remote_copy(src, dst, send, recv, device_id=to, device_id_type=MESH)


def attend_part(q, k_ref, v_ref, starts, cols, top, acc):
    for start in starts:
        part = pl.ds(start, K_BLOCK)
        k, v = k_ref[part, cols], v_ref[part, cols]
        s = lax.dot_general(
            q,
            jnp.concatenate([k, k], axis=1),
            (((1,), (1,)), ((), ())),
            preferred_element_type=jnp.float32,
        )
        here = jnp.max(s, axis=1, keepdims=True)
        peak = here if top is None else jnp.maximum(top, here)
        w = jnp.exp2(s - peak).astype(jnp.bfloat16)
        both = jnp.concatenate([v, jnp.ones_like(v)], axis=1)
        r = jnp.dot(w, both, preferred_element_type=jnp.float32)
        acc = r if top is None else acc * jnp.exp2(top - peak) + r
        top = peak
    return top, acc


def kernel(
    hid_in, q_in, k_in, v_in, k_old, v_old, w_in,
    next_out, guided_out,
    qs, ks, vs, tops, accs, feat, wr, ws, part, rs, rsum, fin, hid, bo, gx, gd,
    q_s, q_r, k_s, k_r, v_s, v_r, w_s, w_r, wx_s, wx_r,
    ag_s, ag_r, rs_s, rs_r, fin_s, fin_r, z_s, z_r, g_s, g_r, loc, out_sem,
):
    me = lax.axis_index("sp")
    core = lax.axis_index("cfg")
    sec = lax.axis_index("pipe")
    sections = lax.axis_size("pipe")
    x, y = lax.div(me, SIDE), lax.rem(me, SIDE)
    behind = lax.rem(sec + 1, sections)
    before = lax.rem(sec + sections - 1, sections)

    def peer(n):
        return lax.rem(me + n, PEERS)

    def x_peer(d):
        return lax.rem(x + d, SIDE)

    def y_peer(d):
        return lax.rem(y + d, SIDE)

    old = pl.ds(FRESH, STALE)
    locals_ = [
        pltpu.make_async_copy(k_old, ks.at[old], loc.at[0]),
        pltpu.make_async_copy(v_old, vs.at[old], loc.at[1]),
        pltpu.make_async_copy(q_in.at[:, :, pl.ds(pl.multiple_of(me * FEAT, FEAT), FEAT)], qs.at[:, me], loc.at[2]),
        pltpu.make_async_copy(k_in.at[:, pl.ds(pl.multiple_of(me * FEAT, FEAT), FEAT)], ks.at[pl.ds(pl.multiple_of(me * 64, 64), 64)], loc.at[3]),
        pltpu.make_async_copy(v_in.at[:, pl.ds(pl.multiple_of(me * FEAT, FEAT), FEAT)], vs.at[pl.ds(pl.multiple_of(me * 64, 64), 64)], loc.at[4]),
        pltpu.make_async_copy(w_in.at[pl.ds(pl.multiple_of(x * WIDE, WIDE), WIDE)], wr.at[x], loc.at[5]),
        pltpu.make_async_copy(hid_in, hid, loc.at[6]),
    ]

    def q_copy(n):
        to = peer(n)
        return remote(q_in.at[:, :, pl.ds(pl.multiple_of(to * FEAT, FEAT), FEAT)], qs.at[:, me], q_s.at[n - 1], q_r.at[n - 1], sp=to)

    def k_copy(n):
        to = peer(n)
        return remote(k_in.at[:, pl.ds(pl.multiple_of(to * FEAT, FEAT), FEAT)], ks.at[pl.ds(pl.multiple_of(me * 64, 64), 64)], k_s.at[n - 1], k_r.at[n - 1], sp=to)

    def v_copy(n):
        to = peer(n)
        return remote(v_in.at[:, pl.ds(pl.multiple_of(to * FEAT, FEAT), FEAT)], vs.at[pl.ds(pl.multiple_of(me * 64, 64), 64)], v_s.at[n - 1], v_r.at[n - 1], sp=to)

    half = pl.ds(pl.multiple_of(core * (WIDE // 2), WIDE // 2), WIDE // 2)

    def w_copy(d):
        to = x_peer(d)
        rows = pl.ds(pl.multiple_of(to * WIDE + core * (WIDE // 2), WIDE // 2), WIDE // 2)
        return remote(w_in.at[rows], wr.at[x, half], w_s.at[d - 1], w_r.at[d - 1], sp=to * SIDE + y)

    def w_cross(d):
        source = x_peer(SIDE - d)
        return remote(wr.at[source, half], wr.at[source, half], wx_s.at[d - 1], wx_r.at[d - 1], cfg=1 - core)

    def ag_copy(b, d):
        return remote(feat.at[b, y], feat.at[b, y], ag_s.at[b, d - 1], ag_r.at[b, d - 1], sp=x * SIDE + y_peer(d))

    def rs_copy(b, d):
        to = x_peer(d)
        rows = pl.ds(pl.multiple_of(to * 64, 64), 64)
        return remote(part.at[b, rows], rs.at[b, d - 1], rs_s.at[b, d - 1], rs_r.at[b, d - 1], sp=to * SIDE + y)

    def fin_copy(b, d):
        to = y_peer(d)
        return remote(rsum.at[b, to], fin.at[b, y], fin_s.at[b, d - 1], fin_r.at[b, d - 1], sp=x * SIDE + to)

    def z_copy(b):
        return remote(bo.at[b], next_out.at[b], z_s.at[b], z_r.at[b], pipe=behind)

    def g_copy(b):
        theirs = pl.ds(pl.multiple_of((1 - core) * HALF, HALF), HALF)
        return remote(bo.at[b, :, theirs], gx.at[b], g_s.at[b], g_r.at[b], cfg=1 - core)

    def each(low, high, act):
        def step(n, carry):
            act(n)
            return carry

        lax.fori_loop(low, high, step, 0)

    for copy in locals_:
        copy.start()

    barrier = pltpu.get_barrier_semaphore()
    each(1, PEERS, lambda n: pl.semaphore_signal(barrier, inc=1, device_id={"sp": peer(n)}, device_id_type=MESH))
    pl.semaphore_signal(barrier, inc=1, device_id={"cfg": 1 - core}, device_id_type=MESH)
    pl.semaphore_signal(barrier, inc=1, device_id={"pipe": behind}, device_id_type=MESH)
    pl.semaphore_signal(barrier, inc=1, device_id={"pipe": before}, device_id_type=MESH)
    pl.semaphore_wait(barrier, PEERS + 2)

    each(1, PEERS, lambda n: q_copy(n).start())
    for copy in locals_:
        copy.wait()
    each(1, PEERS, lambda n: q_copy(n).wait_recv())

    def send_kv(n):
        k_copy(n).start()
        v_copy(n).start()

    each(1, PEERS, send_kv)

    def queries(b, cols):
        scaled = qs[b, :, :, cols].reshape(ROWS, HEAD_DIM).astype(jnp.float32) * SCALE
        high = scaled.astype(jnp.bfloat16)
        low = (scaled - high.astype(jnp.float32)).astype(jnp.bfloat16)
        return jnp.concatenate([high, low], axis=1)

    def stale(b):
        for h in range(2):
            cols = slice(h * HEAD_DIM, (h + 1) * HEAD_DIM)
            top, acc = attend_part(queries(b, cols), ks, vs, range(FRESH, FRESH + STALE, K_BLOCK), cols, None, None)
            tops[b, h] = jnp.broadcast_to(top, (ROWS, HEAD_DIM))
            accs[b, h] = acc

    def fresh(b):
        for h in range(2):
            cols = slice(h * HEAD_DIM, (h + 1) * HEAD_DIM)
            top, acc = attend_part(queries(b, cols), ks, vs, [0], cols, tops[b, h][:, :1], accs[b, h])
            out = acc[:, :HEAD_DIM] / acc[:, HEAD_DIM:]
            feat[b, y, :, cols] = out.astype(jnp.bfloat16)
        each(1, SIDE, lambda d: ag_copy(b, d).start())

    def weights():
        each(1, SIDE, lambda d: w_cross(d).wait_recv())
        chunk = 128

        def lay(i, carry):
            rows = pl.ds(pl.multiple_of(i * chunk, chunk), chunk)
            for s in range(SIDE):
                ws[rows, s * SLICE : (s + 1) * SLICE] = wr[s, rows]
            return carry

        lax.fori_loop(0, WIDE // chunk, lay, 0)

    def project(b):
        each(1, SIDE, lambda d: ag_copy(b, d).wait_recv())
        a = jnp.concatenate([feat[b, i] for i in range(SIDE)], axis=1)
        for n in range(0, COLS, 256):
            r = jnp.dot(a, ws[:, n : n + 256], preferred_element_type=jnp.float32)
            part[b, :, n : n + 256] = r.astype(jnp.bfloat16)
        each(1, SIDE, lambda d: rs_copy(b, d).start())

    def reduce(b):
        each(1, SIDE, lambda d: rs_copy(b, d).wait_recv())
        total = part[b, pl.ds(pl.multiple_of(x * 64, 64), 64)].astype(jnp.float32)
        for d in range(SIDE - 1):
            total = total + rs[b, d].astype(jnp.float32)
        rsum[b] = total.astype(jnp.bfloat16).reshape(SIDE, OWN, COLS)
        fin[b, y] = rsum[b, y]
        each(1, SIDE, lambda d: fin_copy(b, d).start())

    def finish(b):
        each(1, SIDE, lambda d: fin_copy(b, d).wait_recv())
        for s in range(SIDE):
            proj = jnp.concatenate([fin[b, i, :, s * SLICE : (s + 1) * SLICE] for i in range(SIDE)], axis=1)
            wide = slice(s * COLS, (s + 1) * COLS)
            bo[b, :, wide] = (hid[b, :, wide].astype(jnp.float32) + proj.astype(jnp.float32)).astype(jnp.bfloat16)
        z_copy(b).start()
        g_copy(b).start()

    def guide(b):
        g_copy(b).wait_recv()
        own = bo[b, :, pl.ds(pl.multiple_of(core * HALF, HALF), HALF)].astype(jnp.float32)
        other = gx[b].astype(jnp.float32)
        first = core == 0
        cond = jnp.where(first, own, other)
        uncond = jnp.where(first, other, own)
        gd[b] = (uncond + GUIDANCE * (cond - uncond)).astype(jnp.bfloat16)
        pltpu.make_async_copy(gd.at[b], guided_out.at[b], out_sem.at[b]).start()

    def step(t, carry):
        @pl.when(t < BLOCKS)
        def _():
            stale(t)

        @pl.when(t == 0)
        def _():
            each(1, SIDE, lambda d: w_copy(d).start())

        @pl.when(t == 1)
        def _():
            def got(n):
                k_copy(n).wait_recv()
                v_copy(n).wait_recv()

            each(1, PEERS, got)
            fresh(0)

        @pl.when((t >= 1) & (t < BLOCKS))
        def _():
            fresh(t)

        @pl.when(t == 2)
        def _():
            def cross(d):
                w_copy(d).wait_recv()
                w_cross(d).start()

            each(1, SIDE, cross)
            weights()

        @pl.when((t >= 2) & (t < BLOCKS + 2))
        def _():
            project(t - 2)

        @pl.when((t >= 3) & (t < BLOCKS + 3))
        def _():
            reduce(t - 3)

        @pl.when((t >= 4) & (t < BLOCKS + 4))
        def _():
            finish(t - 4)

        @pl.when(t >= 5)
        def _():
            guide(t - 5)

        return carry

    lax.fori_loop(0, BLOCKS + 5, step, 0)

    def sent(n):
        q_copy(n).wait_send()
        k_copy(n).wait_send()
        v_copy(n).wait_send()

    each(1, PEERS, sent)

    def sent_w(d):
        w_copy(d).wait_send()
        w_cross(d).wait_send()

    each(1, SIDE, sent_w)

    def sent_block(b):
        def sent_peer(d):
            ag_copy(b, d).wait_send()
            rs_copy(b, d).wait_send()
            fin_copy(b, d).wait_send()

        each(1, SIDE, sent_peer)
        z_copy(b).wait()
        g_copy(b).wait_send()
        pltpu.make_async_copy(gd.at[b], guided_out.at[b], out_sem.at[b]).wait()

    each(0, BLOCKS, sent_block)


def on_device(hidden, query, key_new, value_new, stale_key, stale_value, out_weight):
    bf16, f32 = jnp.bfloat16, jnp.float32
    vmem, dma = pltpu.VMEM, pltpu.SemaphoreType.DMA
    handed, guided = pl.pallas_call(
        kernel,
        out_shape=(
            jax.ShapeDtypeStruct((BLOCKS, OWN, MODEL), bf16),
            jax.ShapeDtypeStruct((BLOCKS, OWN, HALF), bf16),
        ),
        in_specs=[pl.BlockSpec(memory_space=pl.ANY)] * 7,
        out_specs=(pl.BlockSpec(memory_space=pl.ANY),) * 2,
        scratch_shapes=[
            vmem((BLOCKS, PEERS, OWN, FEAT), bf16),
            vmem((FRESH + STALE, FEAT), bf16),
            vmem((FRESH + STALE, FEAT), bf16),
            vmem((BLOCKS, 2, ROWS, HEAD_DIM), f32),
            vmem((BLOCKS, 2, ROWS, 2 * HEAD_DIM), f32),
            vmem((BLOCKS, SIDE, ROWS, FEAT), bf16),
            vmem((SIDE, WIDE, SLICE), bf16),
            vmem((WIDE, COLS), bf16),
            vmem((BLOCKS, ROWS, COLS), bf16),
            vmem((BLOCKS, SIDE - 1, 64, COLS), bf16),
            vmem((BLOCKS, SIDE, OWN, COLS), bf16),
            vmem((BLOCKS, SIDE, OWN, COLS), bf16),
            vmem((BLOCKS, OWN, MODEL), bf16),
            vmem((BLOCKS, OWN, MODEL), bf16),
            vmem((BLOCKS, OWN, HALF), bf16),
            vmem((BLOCKS, OWN, HALF), bf16),
        ]
        + [dma((PEERS - 1,))] * 6
        + [dma((SIDE - 1,))] * 4
        + [dma((BLOCKS, SIDE - 1))] * 6
        + [dma((BLOCKS,))] * 4
        + [dma((7,)), dma((BLOCKS,))],
        compiler_params=pltpu.CompilerParams(collective_id=0, has_side_effects=True, vmem_limit_bytes=56 * 2**20),
    )(
        hidden.reshape(BLOCKS, OWN, MODEL),
        query.reshape(BLOCKS, OWN, PEERS * FEAT),
        key_new[0, 0],
        value_new[0, 0],
        stale_key[0, 0],
        stale_value[0, 0],
        out_weight[0],
    )
    return (handed.reshape(1, 1, BLOCKS * OWN, MODEL), guided.reshape(1, BLOCKS * OWN, HALF))


def solution(mesh):
    return jax.shard_map(
        on_device,
        mesh=mesh,
        in_specs=(
            P("cfg", "pipe", "sp", None),
            P("cfg", "pipe", "sp", None),
            P("cfg", "pipe", "sp", None),
            P("cfg", "pipe", "sp", None),
            P("cfg", "pipe", None, "sp"),
            P("cfg", "pipe", None, "sp"),
            P("pipe", None, "sp"),
        ),
        out_specs=(P("cfg", "pipe", "sp", None), P("pipe", "sp", "cfg")),
        check_vma=False,
    )
```

```python
import functools

import jax
import jax.numpy as jnp
from jax import lax
from jax.experimental import pallas as pl
from jax.experimental.pallas import tpu as pltpu
from jax.sharding import PartitionSpec as P

HEAD_DIM = 128
SCALE = 1.4426950408889634 / HEAD_DIM**0.5
GUIDANCE = 5.0
MESH = pl.DeviceIdType.MESH
SIDE = 4
PEERS = SIDE * SIDE
BLOCKS = 4
OWN = 16
ROWS = PEERS * OWN
FEAT = 256
WIDE = SIDE * FEAT
SLICE = 320
COLS = SIDE * SLICE
MODEL = PEERS * SLICE
HALF = MODEL // 2
FRESH = 1024
STALE = 7168
K_BLOCK = 1024
W_PARTS = 4
W_AT = 1
W_ROWS = SLICE // W_PARTS


def remote(src, dst, send, recv, **to):
    return pltpu.make_async_remote_copy(src, dst, send, recv, device_id=to, device_id_type=MESH)


def attend_part(q, k_ref, v_ref, starts, cols, top, acc):
    for start in starts:
        part = pl.ds(start, K_BLOCK)
        k, v = k_ref[part, cols], v_ref[part, cols]
        s = lax.dot_general(
            q,
            jnp.concatenate([k, k], axis=1),
            (((1,), (1,)), ((), ())),
            preferred_element_type=jnp.float32,
        )
        here = jnp.max(s, axis=1, keepdims=True)
        peak = here if top is None else jnp.maximum(top, here)
        w = jnp.exp2(s - peak).astype(jnp.bfloat16)
        both = jnp.concatenate([v, jnp.ones_like(v)], axis=1)
        r = jnp.dot(w, both, preferred_element_type=jnp.float32)
        acc = r if top is None else acc * jnp.exp2(top - peak) + r
        top = peak
    return top, acc


def kernel(
    hid_in, q_in, k_in, v_in, k_old, v_old, w_in,
    next_out, guided_out,
    qs, ks, vs, tops, accs, feat, ws, part, far, near, rsum, fin, hid, bo, gx, gd,
    q_s, q_r, k_s, k_r, v_s, v_r, w_s, w_r, wx_s, wx_r,
    ag_s, ag_r, far_s, far_r, near_s, near_r, fin_s, fin_r, z_s, z_r, g_s, g_r, loc, out_sem,
):
    me = lax.axis_index("sp")
    core = lax.axis_index("cfg")
    sec = lax.axis_index("pipe")
    sections = lax.axis_size("pipe")
    x, y = lax.div(me, SIDE), lax.rem(me, SIDE)
    behind = lax.rem(sec + 1, sections)
    before = lax.rem(sec + sections - 1, sections)

    def peer(n):
        return lax.rem(me + n, PEERS)

    def x_peer(d):
        return lax.rem(x + d, SIDE)

    def y_peer(d):
        return lax.rem(y + d, SIDE)

    old = pl.ds(FRESH, STALE)
    locals_ = [
        pltpu.make_async_copy(k_old, ks.at[old], loc.at[0]),
        pltpu.make_async_copy(v_old, vs.at[old], loc.at[1]),
        pltpu.make_async_copy(q_in.at[:, :, pl.ds(pl.multiple_of(me * FEAT, FEAT), FEAT)], qs.at[:, me], loc.at[2]),
        pltpu.make_async_copy(k_in.at[:, pl.ds(pl.multiple_of(me * FEAT, FEAT), FEAT)], ks.at[pl.ds(pl.multiple_of(me * 64, 64), 64)], loc.at[3]),
        pltpu.make_async_copy(v_in.at[:, pl.ds(pl.multiple_of(me * FEAT, FEAT), FEAT)], vs.at[pl.ds(pl.multiple_of(me * 64, 64), 64)], loc.at[4]),
        pltpu.make_async_copy(w_in.at[:, pl.ds(pl.multiple_of(x * WIDE, WIDE), WIDE)], ws.at[x], loc.at[5]),
        pltpu.make_async_copy(hid_in, hid, loc.at[6]),
    ]

    def q_copy(n):
        to = peer(n)
        return remote(q_in.at[:, :, pl.ds(pl.multiple_of(to * FEAT, FEAT), FEAT)], qs.at[:, me], q_s.at[n - 1], q_r.at[n - 1], sp=to)

    def k_copy(n):
        to = peer(n)
        return remote(k_in.at[:, pl.ds(pl.multiple_of(to * FEAT, FEAT), FEAT)], ks.at[pl.ds(pl.multiple_of(me * 64, 64), 64)], k_s.at[n - 1], k_r.at[n - 1], sp=to)

    def v_copy(n):
        to = peer(n)
        return remote(v_in.at[:, pl.ds(pl.multiple_of(to * FEAT, FEAT), FEAT)], vs.at[pl.ds(pl.multiple_of(me * 64, 64), 64)], v_s.at[n - 1], v_r.at[n - 1], sp=to)

    half = pl.ds(pl.multiple_of(core * (WIDE // 2), WIDE // 2), WIDE // 2)

    def w_copy(p, d):
        to = x_peer(d)
        rows = pl.ds(pl.multiple_of(p * W_ROWS, W_ROWS), W_ROWS)
        cols = pl.ds(pl.multiple_of(to * WIDE + core * (WIDE // 2), WIDE // 2), WIDE // 2)
        return remote(w_in.at[rows, cols], ws.at[x, rows, half], w_s.at[p, d - 1], w_r.at[p, d - 1], sp=to * SIDE + y)

    def w_cross(p, d):
        rows = pl.ds(pl.multiple_of(p * W_ROWS, W_ROWS), W_ROWS)
        piece = ws.at[x_peer(SIDE - d), rows, half]
        return remote(piece, piece, wx_s.at[p, d - 1], wx_r.at[p, d - 1], cfg=1 - core)

    def ag_copy(b, d):
        return remote(feat.at[b, y], feat.at[b, y], ag_s.at[b, d - 1], ag_r.at[b, d - 1], sp=x * SIDE + y_peer(d))

    def rows_of(to, start, size):
        return pl.ds(pl.multiple_of(to * 64 + start, size), size)

    def far_copy(b, way):
        rows = rows_of(x_peer(2), 32 * way, 32)
        return remote(part.at[b, rows], far.at[b, way], far_s.at[b, way], far_r.at[b, way], sp=x_peer(1 + 2 * way) * SIDE + y)

    def near_copy(b, way):
        to = x_peer(1 + 2 * way)
        return remote(part.at[b, rows_of(to, 0, 64)], near.at[b, way], near_s.at[b, way], near_r.at[b, way], sp=to * SIDE + y)

    def fin_copy(b, d):
        to = y_peer(d)
        return remote(rsum.at[b, to], fin.at[b, y], fin_s.at[b, d - 1], fin_r.at[b, d - 1], sp=x * SIDE + to)

    def z_copy(b):
        return remote(bo.at[b], next_out.at[b], z_s.at[b], z_r.at[b], pipe=behind)

    def g_copy(b):
        theirs = pl.ds(pl.multiple_of((1 - core) * HALF, HALF), HALF)
        return remote(bo.at[b, :, theirs], gx.at[b], g_s.at[b], g_r.at[b], cfg=1 - core)

    def each(low, high, act):
        def step(n, carry):
            act(n)
            return carry

        lax.fori_loop(low, high, step, 0)

    for copy in locals_:
        copy.start()

    barrier = pltpu.get_barrier_semaphore()
    each(1, PEERS, lambda n: pl.semaphore_signal(barrier, inc=1, device_id={"sp": peer(n)}, device_id_type=MESH))
    pl.semaphore_signal(barrier, inc=1, device_id={"cfg": 1 - core}, device_id_type=MESH)
    pl.semaphore_signal(barrier, inc=1, device_id={"pipe": behind}, device_id_type=MESH)
    pl.semaphore_signal(barrier, inc=1, device_id={"pipe": before}, device_id_type=MESH)
    pl.semaphore_wait(barrier, PEERS + 2)

    each(1, PEERS, lambda n: q_copy(n).start())
    for copy in locals_:
        copy.wait()
    each(1, PEERS, lambda n: q_copy(n).wait_recv())

    def send_kv(n):
        k_copy(n).start()
        v_copy(n).start()

    each(1, PEERS, send_kv)

    def queries(b, cols):
        scaled = qs[b, :, :, cols].reshape(ROWS, HEAD_DIM).astype(jnp.float32) * SCALE
        high = scaled.astype(jnp.bfloat16)
        low = (scaled - high.astype(jnp.float32)).astype(jnp.bfloat16)
        return jnp.concatenate([high, low], axis=1)

    def stale(b):
        for h in range(2):
            cols = slice(h * HEAD_DIM, (h + 1) * HEAD_DIM)
            top, acc = attend_part(queries(b, cols), ks, vs, range(FRESH, FRESH + STALE, K_BLOCK), cols, None, None)
            tops[b, h] = jnp.broadcast_to(top, (ROWS, HEAD_DIM))
            accs[b, h] = acc

    def fresh(b):
        for h in range(2):
            cols = slice(h * HEAD_DIM, (h + 1) * HEAD_DIM)
            top, acc = attend_part(queries(b, cols), ks, vs, [0], cols, tops[b, h][:, :1], accs[b, h])
            out = acc[:, :HEAD_DIM] / acc[:, HEAD_DIM:]
            feat[b, y, :, cols] = out.astype(jnp.bfloat16)
        each(1, SIDE, lambda d: ag_copy(b, d).start())

    def project(b):
        each(1, SIDE, lambda d: ag_copy(b, d).wait_recv())
        a = jnp.concatenate([feat[b, i] for i in range(SIDE)], axis=1)
        w = ws[...].reshape(COLS, WIDE)
        for n in range(0, COLS, 256):
            r = lax.dot_general(
                a, w[n : n + 256], (((1,), (1,)), ((), ())), preferred_element_type=jnp.float32
            )
            part[b, :, n : n + 256] = r.astype(jnp.bfloat16)
        far_copy(b, 0).start()
        far_copy(b, 1).start()

    def merge(b):
        for way in range(2):
            far_copy(b, way).wait_recv()
            rows = rows_of(x_peer(1 + 2 * way), 32 * way, 32)
            both = part[b, rows].astype(jnp.float32) + far[b, way].astype(jnp.float32)
            part[b, rows] = both.astype(jnp.bfloat16)
            near_copy(b, way).start()

    def reduce(b):
        total = part[b, rows_of(x, 0, 64)].astype(jnp.float32)
        for way in range(2):
            near_copy(b, way).wait_recv()
            total = total + near[b, way].astype(jnp.float32)
        rsum[b] = total.astype(jnp.bfloat16).reshape(SIDE, OWN, COLS)
        fin[b, y] = rsum[b, y]
        each(1, SIDE, lambda d: fin_copy(b, d).start())

    def finish(b):
        each(1, SIDE, lambda d: fin_copy(b, d).wait_recv())
        for s in range(SIDE):
            proj = jnp.concatenate([fin[b, i, :, s * SLICE : (s + 1) * SLICE] for i in range(SIDE)], axis=1)
            wide = slice(s * COLS, (s + 1) * COLS)
            bo[b, :, wide] = (hid[b, :, wide].astype(jnp.float32) + proj.astype(jnp.float32)).astype(jnp.bfloat16)
        z_copy(b).start()
        g_copy(b).start()

    def guide(b):
        g_copy(b).wait_recv()
        own = bo[b, :, pl.ds(pl.multiple_of(core * HALF, HALF), HALF)].astype(jnp.float32)
        other = gx[b].astype(jnp.float32)
        first = core == 0
        cond = jnp.where(first, own, other)
        uncond = jnp.where(first, other, own)
        gd[b] = (uncond + GUIDANCE * (cond - uncond)).astype(jnp.bfloat16)
        pltpu.make_async_copy(gd.at[b], guided_out.at[b], out_sem.at[b]).start()

    def got(n):
        k_copy(n).wait_recv()
        v_copy(n).wait_recv()

    def sent(n):
        q_copy(n).wait_send()
        k_copy(n).wait_send()
        v_copy(n).wait_send()

    def parts(act):
        each(0, W_PARTS, lambda p: each(1, SIDE, lambda d: act(p, d)))

    def cross(p, d):
        w_copy(p, d).wait_recv()
        w_cross(p, d).start()

    def attend(b, carry):
        stale(b)

        @pl.when(b == W_AT)
        def _():
            parts(lambda p, d: w_copy(p, d).start())

        @pl.when(b == 1)
        def _():
            each(1, PEERS, got)
            fresh(0)

        @pl.when(b >= 1)
        def _():
            fresh(b)

        return carry

    lax.fori_loop(0, BLOCKS, attend, 0)
    each(1, PEERS, sent)
    parts(cross)
    parts(lambda p, d: w_cross(p, d).wait_recv())

    def step(t, carry):
        for lag, act in enumerate((project, merge, reduce, finish, guide)):

            @pl.when((t >= lag) & (t < BLOCKS + lag))
            def _():
                act(t - lag)

        return carry

    lax.fori_loop(0, BLOCKS + 4, step, 0)

    def sent_w(p, d):
        w_copy(p, d).wait_send()
        w_cross(p, d).wait_send()

    parts(sent_w)

    def sent_block(b):
        def sent_peer(d):
            ag_copy(b, d).wait_send()
            fin_copy(b, d).wait_send()

        each(1, SIDE, sent_peer)
        for way in range(2):
            far_copy(b, way).wait_send()
            near_copy(b, way).wait_send()
        z_copy(b).wait()
        g_copy(b).wait_send()
        pltpu.make_async_copy(gd.at[b], guided_out.at[b], out_sem.at[b]).wait()

    each(0, BLOCKS, sent_block)


def on_device(hidden, query, key_new, value_new, stale_key, stale_value, out_weight):
    bf16, f32 = jnp.bfloat16, jnp.float32
    vmem, dma = pltpu.VMEM, pltpu.SemaphoreType.DMA
    handed, guided = pl.pallas_call(
        kernel,
        out_shape=(
            jax.ShapeDtypeStruct((BLOCKS, OWN, MODEL), bf16),
            jax.ShapeDtypeStruct((BLOCKS, OWN, HALF), bf16),
        ),
        in_specs=[pl.BlockSpec(memory_space=pl.ANY)] * 7,
        out_specs=(pl.BlockSpec(memory_space=pl.ANY),) * 2,
        scratch_shapes=[
            vmem((BLOCKS, PEERS, OWN, FEAT), bf16),
            vmem((FRESH + STALE, FEAT), bf16),
            vmem((FRESH + STALE, FEAT), bf16),
            vmem((BLOCKS, 2, ROWS, HEAD_DIM), f32),
            vmem((BLOCKS, 2, ROWS, 2 * HEAD_DIM), f32),
            vmem((BLOCKS, SIDE, ROWS, FEAT), bf16),
            vmem((SIDE, SLICE, WIDE), bf16),
            vmem((BLOCKS, ROWS, COLS), bf16),
            vmem((BLOCKS, 2, 32, COLS), bf16),
            vmem((BLOCKS, 2, 64, COLS), bf16),
            vmem((BLOCKS, SIDE, OWN, COLS), bf16),
            vmem((BLOCKS, SIDE, OWN, COLS), bf16),
            vmem((BLOCKS, OWN, MODEL), bf16),
            vmem((BLOCKS, OWN, MODEL), bf16),
            vmem((BLOCKS, OWN, HALF), bf16),
            vmem((BLOCKS, OWN, HALF), bf16),
        ]
        + [dma((PEERS - 1,))] * 6
        + [dma((W_PARTS, SIDE - 1))] * 4
        + [dma((BLOCKS, SIDE - 1))] * 2
        + [dma((BLOCKS, 2))] * 4
        + [dma((BLOCKS, SIDE - 1))] * 2
        + [dma((BLOCKS,))] * 4
        + [dma((7,)), dma((BLOCKS,))],
        compiler_params=pltpu.CompilerParams(collective_id=0, has_side_effects=True, vmem_limit_bytes=56 * 2**20),
    )(
        hidden.reshape(BLOCKS, OWN, MODEL),
        query.reshape(BLOCKS, OWN, PEERS * FEAT),
        key_new[0, 0],
        value_new[0, 0],
        stale_key[0, 0],
        stale_value[0, 0],
        out_weight[0].T,
    )
    return (handed.reshape(1, 1, BLOCKS * OWN, MODEL), guided.reshape(1, BLOCKS * OWN, HALF))


def solution(mesh):
    return jax.shard_map(
        on_device,
        mesh=mesh,
        in_specs=(
            P("cfg", "pipe", "sp", None),
            P("cfg", "pipe", "sp", None),
            P("cfg", "pipe", "sp", None),
            P("cfg", "pipe", "sp", None),
            P("cfg", "pipe", None, "sp"),
            P("cfg", "pipe", None, "sp"),
            P("pipe", None, "sp"),
        ),
        out_specs=(P("cfg", "pipe", "sp", None), P("pipe", "sp", "cfg")),
        check_vma=False,
    )
```

```python
import functools

import jax
import jax.numpy as jnp
from jax import lax
from jax.experimental import pallas as pl
from jax.experimental.pallas import tpu as pltpu
from jax.sharding import PartitionSpec as P

HEAD_DIM = 128
SCALE = 1.4426950408889634 / HEAD_DIM**0.5
GUIDANCE = 5.0
MESH = pl.DeviceIdType.MESH
SIDE = 4
PEERS = SIDE * SIDE
BLOCKS = 4
OWN = 16
ROWS = PEERS * OWN
FEAT = 256
WIDE = SIDE * FEAT
SLICE = 320
COLS = SIDE * SLICE
MODEL = PEERS * SLICE
HALF = MODEL // 2
FRESH = 1024
STALE = 7168
K_BLOCK = 1024
W_PARTS = 4
W_ROWS = SLICE // W_PARTS
PARTS = 2
PAIR = SIDE // PARTS
PCOLS = PAIR * SLICE
UNITS = PARTS * BLOCKS


def remote(src, dst, send, recv, **to):
    return pltpu.make_async_remote_copy(src, dst, send, recv, device_id=to, device_id_type=MESH)


def attend_part(q, k_ref, v_ref, starts, cols, top, acc):
    for start in starts:
        part = pl.ds(start, K_BLOCK)
        k, v = k_ref[part, cols], v_ref[part, cols]
        s = lax.dot_general(
            q,
            jnp.concatenate([k, k], axis=1),
            (((1,), (1,)), ((), ())),
            preferred_element_type=jnp.float32,
        )
        here = jnp.max(s, axis=1, keepdims=True)
        peak = here if top is None else jnp.maximum(top, here)
        w = jnp.exp2(s - peak).astype(jnp.bfloat16)
        both = jnp.concatenate([v, jnp.ones_like(v)], axis=1)
        r = jnp.dot(w, both, preferred_element_type=jnp.float32)
        acc = r if top is None else acc * jnp.exp2(top - peak) + r
        top = peak
    return top, acc


def kernel(
    hid_in, q_in, k_in, v_in, k_old, v_old, w_in,
    next_out, guided_out,
    qs, ks, vs, tops, accs, feat, ws, part, far, near, rsum, fin, hid, bo, gx, gd,
    q_s, q_r, k_s, k_r, v_s, v_r, w_s, w_r, wx_s, wx_r,
    ag_s, ag_r, far_s, far_r, near_s, near_r, fin_s, fin_r, z_s, z_r, g_s, g_r, loc, out_sem,
):
    me = lax.axis_index("sp")
    core = lax.axis_index("cfg")
    sec = lax.axis_index("pipe")
    sections = lax.axis_size("pipe")
    x, y = lax.div(me, SIDE), lax.rem(me, SIDE)
    behind = lax.rem(sec + 1, sections)
    before = lax.rem(sec + sections - 1, sections)

    def peer(n):
        return lax.rem(me + n, PEERS)

    def x_peer(d):
        return lax.rem(x + d, SIDE)

    def y_peer(d):
        return lax.rem(y + d, SIDE)

    old = pl.ds(FRESH, STALE)
    locals_ = [
        pltpu.make_async_copy(k_old, ks.at[old], loc.at[0]),
        pltpu.make_async_copy(v_old, vs.at[old], loc.at[1]),
        pltpu.make_async_copy(q_in.at[:, :, pl.ds(pl.multiple_of(me * FEAT, FEAT), FEAT)], qs.at[:, me], loc.at[2]),
        pltpu.make_async_copy(k_in.at[:, pl.ds(pl.multiple_of(me * FEAT, FEAT), FEAT)], ks.at[pl.ds(pl.multiple_of(me * 64, 64), 64)], loc.at[3]),
        pltpu.make_async_copy(v_in.at[:, pl.ds(pl.multiple_of(me * FEAT, FEAT), FEAT)], vs.at[pl.ds(pl.multiple_of(me * 64, 64), 64)], loc.at[4]),
        pltpu.make_async_copy(w_in.at[:, pl.ds(pl.multiple_of(x * WIDE, WIDE), WIDE)], ws.at[x], loc.at[5]),
        pltpu.make_async_copy(hid_in, hid, loc.at[6]),
    ]

    def q_copy(n):
        to = peer(n)
        return remote(q_in.at[:, :, pl.ds(pl.multiple_of(to * FEAT, FEAT), FEAT)], qs.at[:, me], q_s.at[n - 1], q_r.at[n - 1], sp=to)

    def k_copy(n):
        to = peer(n)
        return remote(k_in.at[:, pl.ds(pl.multiple_of(to * FEAT, FEAT), FEAT)], ks.at[pl.ds(pl.multiple_of(me * 64, 64), 64)], k_s.at[n - 1], k_r.at[n - 1], sp=to)

    def v_copy(n):
        to = peer(n)
        return remote(v_in.at[:, pl.ds(pl.multiple_of(to * FEAT, FEAT), FEAT)], vs.at[pl.ds(pl.multiple_of(me * 64, 64), 64)], v_s.at[n - 1], v_r.at[n - 1], sp=to)

    half = pl.ds(pl.multiple_of(core * (WIDE // 2), WIDE // 2), WIDE // 2)

    def w_copy(p, d):
        to = x_peer(d)
        rows = pl.ds(pl.multiple_of(p * W_ROWS, W_ROWS), W_ROWS)
        cols = pl.ds(pl.multiple_of(to * WIDE + core * (WIDE // 2), WIDE // 2), WIDE // 2)
        return remote(w_in.at[rows, cols], ws.at[x, rows, half], w_s.at[p, d - 1], w_r.at[p, d - 1], sp=to * SIDE + y)

    def w_cross(p, d):
        rows = pl.ds(pl.multiple_of(p * W_ROWS, W_ROWS), W_ROWS)
        piece = ws.at[x_peer(SIDE - d), rows, half]
        return remote(piece, piece, wx_s.at[p, d - 1], wx_r.at[p, d - 1], cfg=1 - core)

    def ag_copy(b, d):
        return remote(feat.at[b, y], feat.at[b, y], ag_s.at[b, d - 1], ag_r.at[b, d - 1], sp=x * SIDE + y_peer(d))

    def rows_of(to, start, size):
        return pl.ds(pl.multiple_of(to * 64 + start, size), size)

    def far_copy(p, b, way):
        rows = rows_of(x_peer(2), 32 * way, 32)
        to = x_peer(1 + 2 * way) * SIDE + y
        return remote(part.at[p, b, rows], far.at[p, b, way], far_s.at[p, b, way], far_r.at[p, b, way], sp=to)

    def near_copy(p, b, way):
        to = x_peer(1 + 2 * way)
        rows = rows_of(to, 0, 64)
        return remote(part.at[p, b, rows], near.at[p, b, way], near_s.at[p, b, way], near_r.at[p, b, way], sp=to * SIDE + y)

    def fin_copy(p, b, d):
        to = y_peer(d)
        return remote(rsum.at[p, b, to], fin.at[p, b, y], fin_s.at[p, b, d - 1], fin_r.at[p, b, d - 1], sp=x * SIDE + to)

    def z_copy(p, b):
        cols = pl.ds(pl.multiple_of(p * HALF, HALF), HALF)
        return remote(bo.at[b, :, cols], next_out.at[b, :, cols], z_s.at[p, b], z_r.at[p, b], pipe=behind)

    def g_copy(b):
        theirs = pl.ds(pl.multiple_of((1 - core) * HALF, HALF), HALF)
        return remote(bo.at[b, :, theirs], gx.at[b], g_s.at[b], g_r.at[b], cfg=1 - core)

    def guided_copy(b):
        return pltpu.make_async_copy(gd.at[b], guided_out.at[b], out_sem.at[b])

    def each(low, high, act):
        def step(n, carry):
            act(n)
            return carry

        lax.fori_loop(low, high, step, 0)

    for copy in locals_:
        copy.start()

    barrier = pltpu.get_barrier_semaphore()
    each(1, PEERS, lambda n: pl.semaphore_signal(barrier, inc=1, device_id={"sp": peer(n)}, device_id_type=MESH))
    pl.semaphore_signal(barrier, inc=1, device_id={"cfg": 1 - core}, device_id_type=MESH)
    pl.semaphore_signal(barrier, inc=1, device_id={"pipe": behind}, device_id_type=MESH)
    pl.semaphore_signal(barrier, inc=1, device_id={"pipe": before}, device_id_type=MESH)
    pl.semaphore_wait(barrier, PEERS + 2)

    each(1, PEERS, lambda n: q_copy(n).start())
    for copy in locals_:
        copy.wait()
    each(1, PEERS, lambda n: q_copy(n).wait_recv())

    def send_kv(n):
        k_copy(n).start()
        v_copy(n).start()

    each(1, PEERS, send_kv)

    def queries(b, cols):
        scaled = qs[b, :, :, cols].reshape(ROWS, HEAD_DIM).astype(jnp.float32) * SCALE
        high = scaled.astype(jnp.bfloat16)
        low = (scaled - high.astype(jnp.float32)).astype(jnp.bfloat16)
        return jnp.concatenate([high, low], axis=1)

    def stale(b):
        for h in range(2):
            cols = slice(h * HEAD_DIM, (h + 1) * HEAD_DIM)
            top, acc = attend_part(queries(b, cols), ks, vs, range(FRESH, FRESH + STALE, K_BLOCK), cols, None, None)
            tops[b, h] = jnp.broadcast_to(top, (ROWS, HEAD_DIM))
            accs[b, h] = acc

    def fresh(b):
        for h in range(2):
            cols = slice(h * HEAD_DIM, (h + 1) * HEAD_DIM)
            top, acc = attend_part(queries(b, cols), ks, vs, [0], cols, tops[b, h][:, :1], accs[b, h])
            out = acc[:, :HEAD_DIM] / acc[:, HEAD_DIM:]
            feat[b, y, :, cols] = out.astype(jnp.bfloat16)
        each(1, SIDE, lambda d: ag_copy(b, d).start())

    def project(p, b):
        a = jnp.concatenate([feat[b, i] for i in range(SIDE)], axis=1)
        w = ws[pl.ds(p * PAIR, PAIR)].reshape(PCOLS, WIDE)
        for n in range(0, PCOLS, 256):
            cols = slice(n, min(n + 256, PCOLS))
            r = lax.dot_general(a, w[cols], (((1,), (1,)), ((), ())), preferred_element_type=jnp.float32)
            part[p, b, :, cols] = r.astype(jnp.bfloat16)
        far_copy(p, b, 0).start()
        far_copy(p, b, 1).start()

    def merge(p, b):
        for way in range(2):
            far_copy(p, b, way).wait_recv()
            rows = rows_of(x_peer(1 + 2 * way), 32 * way, 32)
            both = part[p, b, rows].astype(jnp.float32) + far[p, b, way].astype(jnp.float32)
            part[p, b, rows] = both.astype(jnp.bfloat16)
            near_copy(p, b, way).start()

    def reduce(p, b):
        total = part[p, b, rows_of(x, 0, 64)].astype(jnp.float32)
        for way in range(2):
            near_copy(p, b, way).wait_recv()
            total = total + near[p, b, way].astype(jnp.float32)
        rsum[p, b] = total.astype(jnp.bfloat16).reshape(SIDE, OWN, PCOLS)
        fin[p, b, y] = rsum[p, b, y]
        each(1, SIDE, lambda d: fin_copy(p, b, d).start())

    def finish(p, b):
        each(1, SIDE, lambda d: fin_copy(p, b, d).wait_recv())
        for s in range(PAIR):
            cols = slice(s * SLICE, (s + 1) * SLICE)
            proj = jnp.concatenate([fin[p, b, i, :, cols] for i in range(SIDE)], axis=1)
            wide = pl.ds(pl.multiple_of((p * PAIR + s) * COLS, COLS), COLS)
            bo[b, :, wide] = (hid[b, :, wide].astype(jnp.float32) + proj.astype(jnp.float32)).astype(jnp.bfloat16)
        z_copy(p, b).start()

        @pl.when(p == 1 - core)
        def _():
            g_copy(b).start()

    def guide(b):
        g_copy(b).wait_recv()
        own = bo[b, :, pl.ds(pl.multiple_of(core * HALF, HALF), HALF)].astype(jnp.float32)
        other = gx[b].astype(jnp.float32)
        first = core == 0
        cond = jnp.where(first, own, other)
        uncond = jnp.where(first, other, own)
        gd[b] = (uncond + GUIDANCE * (cond - uncond)).astype(jnp.bfloat16)
        guided_copy(b).start()

    def got(n):
        k_copy(n).wait_recv()
        v_copy(n).wait_recv()

    def sent(n):
        q_copy(n).wait_send()
        k_copy(n).wait_send()
        v_copy(n).wait_send()

    def parts(act):
        each(0, W_PARTS, lambda p: each(1, SIDE, lambda d: act(p, d)))

    def cross(p, d):
        w_copy(p, d).wait_recv()
        w_cross(p, d).start()

    def attend(b, carry):
        stale(b)

        @pl.when(b == 1)
        def _():
            each(1, PEERS, got)
            parts(lambda p, d: w_copy(p, d).start())
            fresh(0)

        @pl.when(b >= 1)
        def _():
            fresh(b)

        return carry

    lax.fori_loop(0, BLOCKS, attend, 0)
    parts(cross)
    parts(lambda p, d: w_cross(p, d).wait_recv())

    def sent_w(p, d):
        w_copy(p, d).wait_send()
        w_cross(p, d).wait_send()

    def settle(p, b):
        for way in range(2):
            far_copy(p, b, way).wait_send()
            near_copy(p, b, way).wait_send()
        each(1, SIDE, lambda d: fin_copy(p, b, d).wait_send())

        @pl.when(p == 0)
        def _():
            each(1, SIDE, lambda d: ag_copy(b, d).wait_send())

    def step(t, carry):
        @pl.when(t == 4)
        def _():
            each(1, PEERS, sent)

        @pl.when(t == 5)
        def _():
            parts(sent_w)

        @pl.when((t < UNITS) & (lax.rem(t, PARTS) == 0))
        def _():
            b = lax.div(t, PARTS)
            each(1, SIDE, lambda d: ag_copy(b, d).wait_recv())

        for lag, act in ((0, project), (2, merge), (4, reduce), (6, finish), (7, settle)):

            @pl.when((t >= lag) & (t < UNITS + lag))
            def _():
                act(lax.rem(t - lag, PARTS), lax.div(t - lag, PARTS))

        @pl.when((t >= 8) & (lax.rem(t - 7, PARTS) == 1))
        def _():
            guide(lax.div(t - 7, PARTS))

        return carry

    lax.fori_loop(0, UNITS + 7, step, 0)

    def sent_block(b):
        each(0, PARTS, lambda p: z_copy(p, b).wait())
        g_copy(b).wait_send()
        guided_copy(b).wait()

    each(0, BLOCKS, sent_block)


def on_device(hidden, query, key_new, value_new, stale_key, stale_value, out_weight):
    bf16, f32 = jnp.bfloat16, jnp.float32
    vmem, dma = pltpu.VMEM, pltpu.SemaphoreType.DMA
    handed, guided = pl.pallas_call(
        kernel,
        out_shape=(
            jax.ShapeDtypeStruct((BLOCKS, OWN, MODEL), bf16),
            jax.ShapeDtypeStruct((BLOCKS, OWN, HALF), bf16),
        ),
        in_specs=[pl.BlockSpec(memory_space=pl.ANY)] * 7,
        out_specs=(pl.BlockSpec(memory_space=pl.ANY),) * 2,
        scratch_shapes=[
            vmem((BLOCKS, PEERS, OWN, FEAT), bf16),
            vmem((FRESH + STALE, FEAT), bf16),
            vmem((FRESH + STALE, FEAT), bf16),
            vmem((BLOCKS, 2, ROWS, HEAD_DIM), f32),
            vmem((BLOCKS, 2, ROWS, 2 * HEAD_DIM), f32),
            vmem((BLOCKS, SIDE, ROWS, FEAT), bf16),
            vmem((SIDE, SLICE, WIDE), bf16),
            vmem((PARTS, BLOCKS, ROWS, PCOLS), bf16),
            vmem((PARTS, BLOCKS, 2, 32, PCOLS), bf16),
            vmem((PARTS, BLOCKS, 2, 64, PCOLS), bf16),
            vmem((PARTS, BLOCKS, SIDE, OWN, PCOLS), bf16),
            vmem((PARTS, BLOCKS, SIDE, OWN, PCOLS), bf16),
            vmem((BLOCKS, OWN, MODEL), bf16),
            vmem((BLOCKS, OWN, MODEL), bf16),
            vmem((BLOCKS, OWN, HALF), bf16),
            vmem((BLOCKS, OWN, HALF), bf16),
        ]
        + [dma((PEERS - 1,))] * 6
        + [dma((W_PARTS, SIDE - 1))] * 4
        + [dma((BLOCKS, SIDE - 1))] * 2
        + [dma((PARTS, BLOCKS, 2))] * 4
        + [dma((PARTS, BLOCKS, SIDE - 1))] * 2
        + [dma((PARTS, BLOCKS))] * 2
        + [dma((BLOCKS,))] * 2
        + [dma((7,)), dma((BLOCKS,))],
        compiler_params=pltpu.CompilerParams(collective_id=0, has_side_effects=True, vmem_limit_bytes=56 * 2**20),
    )(
        hidden.reshape(BLOCKS, OWN, MODEL),
        query.reshape(BLOCKS, OWN, PEERS * FEAT),
        key_new[0, 0],
        value_new[0, 0],
        stale_key[0, 0],
        stale_value[0, 0],
        out_weight[0].T,
    )
    return (handed.reshape(1, 1, BLOCKS * OWN, MODEL), guided.reshape(1, BLOCKS * OWN, HALF))


def solution(mesh):
    return jax.shard_map(
        on_device,
        mesh=mesh,
        in_specs=(
            P("cfg", "pipe", "sp", None),
            P("cfg", "pipe", "sp", None),
            P("cfg", "pipe", "sp", None),
            P("cfg", "pipe", "sp", None),
            P("cfg", "pipe", None, "sp"),
            P("cfg", "pipe", None, "sp"),
            P("pipe", None, "sp"),
        ),
        out_specs=(P("cfg", "pipe", "sp", None), P("pipe", "sp", "cfg")),
        check_vma=False,
    )
```
